32 devices in a mesh: ctx: 8 (over y, x, core), exp: 4 (over z).
Axes of the slice: x: 2, y: 2, z: 4, core: 2. Of those that a mesh axis runs over, the one named last changes fastest.
Arguments:
- span_q: bfloat16 [1024, 6144], P('ctx', 'exp'), may hold values from -9 to 9
- prompt_kv: bfloat16 [2, 8192, 1024], P(None, 'ctx', 'exp'), may hold values from -10 to 10
- span_kv: bfloat16 [2, 1024, 1024], P(None, 'ctx', 'exp'), may hold values from -10 to 10
- decode_q: bfloat16 [128, 6144], P('ctx', 'exp'), may hold values from -4 to 4
- decode_cache: bfloat16 [2, 128, 256, 1024], P(None, 'ctx', None, 'exp'), may hold values from -10 to 10
- decode_new: bfloat16 [2, 128, 1024], P(None, 'ctx', 'exp'), may hold values from -10.5 to 10.5
- decode_len: int32 [128], P('ctx'), may hold values from 1 to 256, as said below
- residual: bfloat16 [1152, 6144], P('ctx', 'exp'), may hold values from -1.5 to 1.5
- norm_gain: bfloat16 [6144], P('exp'), may hold values from 0.099609375 to 1.8984375
- router: bfloat16 [6144, 8], P('exp'), may hold values from -0.078125 to 0.078125
- expert_ids: int32 [1152, 2], P('ctx'), may hold values from 0 to 7, all different within a row; in each aligned block of 144 rows (0 to 143, 144 to 287, ...) at most 40 rows name the same one
- capacity: int32 [8], replicated, may hold values from 20 to 40, as said below
- w_gate: bfloat16 [8, 6144, 8192], P('exp', None, 'ctx'), may hold values from -0.078125 to 0.078125
- w_up: bfloat16 [8, 6144, 8192], P('exp', None, 'ctx'), may hold values from -0.078125 to 0.078125
- w_down: bfloat16 [8, 8192, 6144], P('exp', 'ctx'), may hold values from -0.0625 to 0.0625
Outputs:
- mixed: bfloat16 [1152, 6144], P('ctx', 'exp')
The draws below stay inside these ranges and needn't reach their ends.
Inputs may be any that keep to these rules, and one draw needn't show every extreme that they name: `decode_len`: some decode row has exactly 256 cached positions. Some expert's capacity is exactly 40. `expert_ids`: in each row block of 144 rows (the rows of one ctx index) no expert is named by more than 40 rows; in some block some expert is named by exactly 40 rows.
All inputs are finite; a program needn't handle non-finite values.
Results may differ from the reference program's by a relative error of at most 0.019.
Values may be sent and summed in bfloat16 or wider, within the bound.
A program may use at most 192 MiB of HBM per device.

```python
import math
import jax
import jax.numpy as jnp
import numpy as np
from jax import lax

D = 6144
HD = 128
QPK = 6
KVH = 8
EXPERTS = 8
TOPK = 2
FF = 8192
SPAN_DEV = 128
DEC_DEV = 16
DEC_LEN = 256
PROMPT = 8192
SPAN = 1024
DECODE = 128
ROWS_DEV = 144
ROWS = 1152
CAP = 40
FF_DEV = 1024
N_CTX = 8


def draw_span_q(key, part):
    key = jax.random.fold_in(key, 5)
    first = jax.random.fold_in(key, 0)
    base = jnp.clip(2.2 * jax.random.normal(first, (SPAN, KVH * QPK, HD), jnp.float32), -9.0, 9.0)
    return base.reshape(SPAN, D).astype(jnp.bfloat16)


def draw_prompt_kv(key, part):
    key = jax.random.fold_in(key, 3)
    base = jnp.clip(jax.random.normal(key, (2, PROMPT, KVH, HD), jnp.float32), -4.0, 4.0)
    return base.reshape(2, PROMPT, KVH * HD).astype(jnp.bfloat16)


def draw_span_kv(key, part):
    key = jax.random.fold_in(key, 29)
    first = jax.random.fold_in(key, 0)
    base = jnp.clip(jax.random.normal(first, (2, SPAN, KVH, HD), jnp.float32), -4.0, 4.0)
    return base.reshape(2, SPAN, KVH * HD).astype(jnp.bfloat16)


def draw_decode_q(key, part):
    key = jax.random.fold_in(key, 17)
    first = jax.random.fold_in(key, 0)
    base = jnp.clip(jax.random.normal(first, (DECODE, KVH * QPK, HD), jnp.float32), -4.0, 4.0)
    return base.reshape(DECODE, D).astype(jnp.bfloat16)


def draw_decode_cache(key, part):
    key = jax.random.fold_in(key, 19)
    base = jnp.clip(jax.random.normal(key, (2, DECODE, DEC_LEN, KVH, HD), jnp.float32), -4.0, 4.0)
    return base.reshape(2, DECODE, DEC_LEN, KVH * HD).astype(jnp.bfloat16)


def draw_decode_new(key, part):
    key = jax.random.fold_in(key, 23)
    base = jnp.clip(jax.random.normal(key, (2, DECODE, KVH, HD), jnp.float32), -4.0, 4.0)
    return base.reshape(2, DECODE, KVH * HD).astype(jnp.bfloat16)


def draw_decode_len(key, part):
    key = jax.random.fold_in(key, 7)
    first, second, third = jax.random.split(key, 3)
    lengths = jnp.minimum(jax.random.randint(first, (DECODE,), 1, DEC_LEN + 1), jax.random.randint(second, (DECODE,), 1, DEC_LEN + 1))
    spot = jax.random.randint(third, (), 0, DECODE)
    return jnp.where(jnp.arange(DECODE) == spot, DEC_LEN, lengths).astype(jnp.int32)


def draw_capacity(key, part):
    key = jax.random.fold_in(key, 11)
    first, second = jax.random.split(key)
    values = jax.random.randint(first, (EXPERTS,), CAP - CAP // 2, CAP + 1)
    spot = jax.random.randint(second, (), 0, EXPERTS)
    return jnp.where(jnp.arange(EXPERTS) == spot, CAP, values).astype(jnp.int32)


def draw_residual(key, part):
    key = jax.random.fold_in(key, 13)
    ramp = jnp.arange(D, dtype=jnp.float32) / D
    values = jnp.clip(jax.random.normal(key, (ROWS, D), jnp.float32), -3.0, 3.0) * jnp.exp(ramp * 1.0986123) * 0.16
    return values.astype(jnp.bfloat16)


def block_levels(key, extent, cuts, low, high):
    def one(dim, blocks):
        heights = jax.random.uniform(jax.random.fold_in(jax.random.fold_in(key, 6), dim), (blocks,), jnp.float32, low / len(cuts), high / len(cuts))
        return jnp.repeat(jnp.exp(heights), extent[dim] // blocks).reshape((-1,) + (1,) * (len(extent) - dim - 1))

    factor_of = one(*cuts[0])
    for cut in cuts[1:]:
        factor_of = factor_of * one(*cut)
    return factor_of


def routed_block(rng, own, number, rows, number_of, top, bound, skew):
    sequence = jax.random.permutation(rng, number_of)
    heavy_load, usual = load_shares(number_of, rows * top, bound, skew, True), load_shares(number_of, rows * top, bound, skew, False)
    places = jnp.arange(number_of)

    def named(tallies, rotation):
        used = int((tallies > 0).sum())
        fixed = max(1, used // 4)
        shifted = fixed + (places - fixed + rotation * (used - fixed)) % max(1, number_of - fixed)
        return jnp.zeros((number_of,), jnp.int32).at[sequence[jnp.where(places < fixed, places, shifted)]].set(jnp.asarray(tallies, jnp.int32))

    tallies = jnp.where(number % 4 == 0, named(heavy_load, number // 4), named(usual, number - number // 4 - 1))
    mixed = jax.random.permutation(jax.random.fold_in(own, 3), number_of)
    donor, sink = mixed[0:number_of // 2 * 2:2], mixed[1:number_of // 2 * 2:2]
    room = jnp.minimum(tallies[donor] - 1, bound - tallies[sink]) // 2
    room = jnp.where((donor == sequence[0]) | (sink == sequence[0]) | (tallies[sink] == 0), 0, jnp.maximum(room, 0))
    shifted = jax.random.randint(jax.random.fold_in(own, 4), (number_of // 2,), 0, 1 << 20) % (room + 1)
    tallies = tallies.at[donor].add(-shifted).at[sink].add(shifted)
    labels = jnp.searchsorted(jnp.cumsum(tallies), jnp.arange(rows * top), side="right").astype(jnp.int32)
    listing = labels.reshape(top, rows).T
    listing = listing[jax.random.permutation(jax.random.fold_in(own, 1), rows)]
    rotation = jax.random.randint(jax.random.fold_in(own, 2), (rows, 1), 0, top)
    return jnp.take_along_axis(listing, (jnp.arange(top)[None, :] + rotation) % top, axis=1)


def load_shares(amount, total, reach, slope, full):
    portions = [(1 << 20) // math.isqrt(standing ** slope) + 1 for standing in range(1, amount + 1)]
    largest = reach if full else min(reach, max(-(-total // amount), total * portions[0] // sum(portions)))
    least = 1 if total - largest >= amount - 1 else 0
    counts, spare = [largest] + [least] * (amount - 1), total - largest - least * (amount - 1)
    while spare > 0:
        candidates = [i for i in range(1, amount) if counts[i] < largest] or [i for i in range(1, amount) if counts[i] < reach]
        whole, left = sum([portions[i] for i in candidates]), spare
        for i in candidates:
            extra = min(reach - counts[i], max(1, left * portions[i] // whole), spare)
            counts[i] = counts[i] + extra
            spare = spare - extra
    return np.array(counts)


def normal_values(rng, extent, width, bound, shards=(), kind=jnp.bfloat16):
    values = jax.random.normal(rng, extent, jnp.float32) * width
    if len(shards) > 0:
        values = block_levels(rng, extent, shards, -0.22, 0.18) * values
    return jnp.clip(values, min=-bound, max=bound).astype(kind)


def setup_inputs(seed: int = 0) -> dict:
    key_of = jax.random.split(jax.random.key(seed), 16)
    span_q = draw_span_q(jax.random.fold_in(key_of[15], 71), 0)
    prompt_kv = draw_prompt_kv(jax.random.fold_in(key_of[15], 71), 0)
    span_kv = draw_span_kv(jax.random.fold_in(key_of[15], 71), 0)
    decode_q = draw_decode_q(jax.random.fold_in(key_of[15], 71), 0)
    decode_cache = draw_decode_cache(jax.random.fold_in(key_of[15], 71), 0)
    decode_new = draw_decode_new(jax.random.fold_in(key_of[15], 71), 0)
    decode_len = draw_decode_len(jax.random.fold_in(key_of[15], 71), 0)
    residual = draw_residual(jax.random.fold_in(key_of[15], 71), 0)
    norm_gain = jnp.clip(1.0 + 0.18 * jax.random.normal(key_of[8], (D,), jnp.float32), 0.099609375, 1.8984375).astype(jnp.bfloat16)
    router = normal_values(key_of[9], (D, EXPERTS), D ** -0.5, 0.078125, ((0, 4),))
    expert_ids_keys = jax.random.split(jax.random.fold_in(key_of[10], 1), ROWS // ROWS_DEV)
    expert_ids_turns = jax.random.permutation(jax.random.fold_in(key_of[10], 3), ROWS // ROWS_DEV)
    expert_ids = jax.vmap(lambda own, number: routed_block(jax.random.fold_in(key_of[10], 2), own, number, ROWS_DEV, EXPERTS, TOPK, CAP, 2))(expert_ids_keys, expert_ids_turns).reshape((ROWS, TOPK))
    capacity = draw_capacity(jax.random.fold_in(key_of[15], 71), 0)
    w_gate = normal_values(key_of[12], (EXPERTS, D, FF), D ** -0.5, 0.078125, ((0, 4), (2, 8)))
    w_up = normal_values(key_of[13], (EXPERTS, D, FF), D ** -0.5, 0.078125, ((0, 4), (2, 8)))
    w_down = normal_values(key_of[14], (EXPERTS, FF, D), FF ** -0.5, 0.0625, ((0, 4), (1, 8)))
    return {"span_q": span_q, "prompt_kv": prompt_kv, "span_kv": span_kv, "decode_q": decode_q, "decode_cache": decode_cache, "decode_new": decode_new, "decode_len": decode_len, "residual": residual, "norm_gain": norm_gain, "router": router, "expert_ids": expert_ids, "capacity": capacity, "w_gate": w_gate, "w_up": w_up, "w_down": w_down}


NEG = -1e+30
EPS = 1e-05

def span_attention(span_q, prompt_kv, span_kv):
    total_keys = PROMPT + SPAN
    keys = jnp.concatenate([prompt_kv[0], span_kv[0]], axis=0).reshape(total_keys, KVH, HD)
    values = jnp.concatenate([prompt_kv[1], span_kv[1]], axis=0).reshape(total_keys, KVH, HD)
    queries = span_q.reshape(SPAN, KVH, QPK, HD)
    key_place = jnp.arange(total_keys, dtype=jnp.int32) - PROMPT
    block = math.gcd(SPAN, 512)
    starts = jnp.arange(SPAN // block, dtype=jnp.int32) * block
    keys_t = jnp.transpose(keys, (1, 0, 2))
    values_t = jnp.transpose(values, (1, 0, 2))
    queries_t = jnp.transpose(queries, (1, 0, 2, 3))

    def one_head(operands):
        head_q, head_k, head_v = operands
        key_float = head_k.astype(jnp.float32)
        value_float = head_v.astype(jnp.float32)

        def one_block(start):
            query_block = lax.dynamic_slice_in_dim(head_q, start, block, 0).astype(jnp.float32)
            scores = jnp.einsum('cqd,kd->cqk', query_block, key_float) * HD ** (-0.5)
            place = start + jnp.arange(block, dtype=jnp.int32)
            visible = (key_place[None, :] <= place[:, None])[:, None, :]
            top = lax.optimization_barrier(jnp.max(jnp.where(visible, scores, NEG), axis=-1, keepdims=True))
            weights = jnp.where(visible, jnp.exp(scores - top), 0.0)
            probs = lax.optimization_barrier(weights.astype(jnp.bfloat16)).astype(jnp.float32)
            summed = jnp.einsum('cqk,kd->cqd', probs, value_float)
            return summed / lax.optimization_barrier(jnp.sum(weights, axis=-1, keepdims=True))
        return lax.map(one_block, starts)
    result = lax.map(one_head, (queries_t, keys_t, values_t))
    result = result.reshape(KVH, SPAN, QPK, HD).transpose(1, 0, 2, 3).reshape(SPAN, D)
    return result.astype(jnp.bfloat16)

def decode_attention(decode_q, decode_cache, decode_new, decode_len):
    queries = decode_q.reshape(DECODE, KVH, QPK, HD).astype(jnp.float32)
    keys = decode_cache[0].reshape(DECODE, DEC_LEN, KVH, HD).astype(jnp.float32)
    values = decode_cache[1].reshape(DECODE, DEC_LEN, KVH, HD).astype(jnp.float32)
    own_key = decode_new[0].reshape(DECODE, KVH, HD).astype(jnp.float32)
    own_value = decode_new[1].reshape(DECODE, KVH, HD).astype(jnp.float32)
    scale = HD ** (-0.5)
    scores = jnp.einsum('rgqd,rlgd->rgql', queries, keys) * scale
    live = (jnp.arange(DEC_LEN, dtype=jnp.int32)[None, :] < decode_len[:, None])[:, None, None, :]
    own = jnp.einsum('rgqd,rgd->rgq', queries, own_key) * scale
    top = jnp.maximum(lax.optimization_barrier(jnp.max(jnp.where(live, scores, NEG), axis=-1)), own)
    weights = jnp.where(live, jnp.exp(scores - top[..., None]), 0.0)
    own_weight = jnp.exp(own - top)
    probs = lax.optimization_barrier(weights.astype(jnp.bfloat16)).astype(jnp.float32)
    own_prob = lax.optimization_barrier(own_weight.astype(jnp.bfloat16)).astype(jnp.float32)
    summed = jnp.einsum('rgql,rlgd->rgqd', probs, values) + own_prob[..., None] * own_value[:, :, None, :]
    result = summed / (lax.optimization_barrier(jnp.sum(weights, axis=-1)) + own_weight)[..., None]
    return result.reshape(DECODE, D).astype(jnp.bfloat16)

def experts(normed, route_weight, expert_ids, capacity, w_gate, w_up, w_down):
    assigns = ROWS_DEV * TOPK
    slots = CAP * EXPERTS
    ids = expert_ids.reshape(N_CTX, assigns)
    onehot = (ids[:, :, None] == jnp.arange(EXPERTS, dtype=jnp.int32)[None, None, :]).astype(jnp.int32)
    prior = jnp.cumsum(onehot, axis=1) - onehot
    position = lax.optimization_barrier(jnp.sum(prior * onehot, axis=-1))
    limit = lax.optimization_barrier(jnp.sum(onehot * capacity[None, None, :], axis=-1))
    kept = position < limit
    slot = position * EXPERTS + ids
    select = kept[:, :, None] & (slot[:, :, None] == jnp.arange(slots, dtype=jnp.int32)[None, None, :])
    select = select.astype(jnp.float32).reshape(N_CTX, ROWS_DEV, TOPK, slots)
    rows = lax.optimization_barrier(normed).astype(jnp.float32).reshape(N_CTX, ROWS_DEV, D)
    placed = jnp.einsum('crs,crd->csd', lax.optimization_barrier(jnp.sum(select, axis=2)), rows).astype(jnp.bfloat16)
    by_expert = placed.reshape(N_CTX, CAP, EXPERTS, D).transpose(2, 0, 1, 3).reshape(EXPERTS, N_CTX * CAP, D)

    def one_expert(operands):
        inputs, gate_w, up_w, down_w = operands
        gate = jnp.dot(inputs, gate_w, preferred_element_type=jnp.float32)
        up = jnp.dot(inputs, up_w, preferred_element_type=jnp.float32)
        hidden = (jax.nn.silu(gate) * up).astype(jnp.bfloat16)
        pieces = hidden.reshape(N_CTX * CAP, N_CTX, FF_DEV).transpose(1, 0, 2)
        downs = down_w.reshape(N_CTX, FF_DEV, D)

        def add_piece(total, operand):
            piece, down_piece = operand
            part = jnp.dot(piece, down_piece, preferred_element_type=jnp.float32).astype(jnp.bfloat16)
            return (total + lax.optimization_barrier(part).astype(jnp.float32), None)
        total, unused = lax.scan(add_piece, jnp.zeros((N_CTX * CAP, D), jnp.float32), (pieces, downs))
        return total.astype(jnp.bfloat16)
    outputs = lax.map(one_expert, (by_expert, w_gate, w_up, w_down))
    back = outputs.reshape(EXPERTS, N_CTX, CAP, D).transpose(1, 2, 0, 3).reshape(N_CTX, slots, D)
    back = lax.optimization_barrier(back).astype(jnp.float32)
    mixing = lax.optimization_barrier(jnp.sum(select * route_weight.reshape(N_CTX, ROWS_DEV, TOPK)[..., None], axis=2))
    moe = jnp.einsum('crs,csd->crd', mixing, back, precision=lax.Precision.HIGHEST)
    return moe.reshape(ROWS, D)

def reference(span_q, prompt_kv, span_kv, decode_q, decode_cache, decode_new, decode_len, residual, norm_gain, router, expert_ids, capacity, w_gate, w_up, w_down):
    span_out = span_attention(span_q, prompt_kv, span_kv)
    decode_out = decode_attention(decode_q, decode_cache, decode_new, decode_len)
    attn = jnp.concatenate([span_out.reshape(N_CTX, SPAN_DEV, D), decode_out.reshape(N_CTX, DEC_DEV, D)], axis=1).reshape(ROWS, D)
    carried = residual.astype(jnp.float32) + lax.optimization_barrier(attn).astype(jnp.float32)
    rscale = lax.rsqrt(lax.optimization_barrier(jnp.sum(carried * carried, axis=1)) / D + EPS)
    gained = carried * norm_gain.astype(jnp.float32)
    logits = jnp.dot(gained, router.astype(jnp.float32), precision=lax.Precision.HIGHEST) * rscale[:, None]
    normed = (gained * rscale[:, None]).astype(jnp.bfloat16)
    onehot = expert_ids[:, :, None] == jnp.arange(EXPERTS, dtype=jnp.int32)[None, None, :]
    chosen = lax.optimization_barrier(jnp.sum(jnp.where(onehot, logits[:, None, :], 0.0), axis=-1))
    route_weight = jax.nn.sigmoid(chosen - chosen[:, ::-1])
    moe = experts(normed, route_weight, expert_ids, capacity, w_gate, w_up, w_down)
    return (carried + moe).astype(jnp.bfloat16)
```

```python
import functools

import jax
import jax.numpy as jnp
from jax import lax
from jax.experimental import pallas as pl
from jax.experimental.pallas import tpu as pltpu
from jax.sharding import PartitionSpec as P

D = 6144
HD = 128
QPK = 6
EXPERTS = 8
TOPK = 2
CAP = 40


NEG = -1e30
EPS = 1e-05


def from_behind(value, axis, steps):
    count = lax.axis_size(axis)
    pairs = [(source, (source + steps) % count) for source in range(count)]
    return lax.ppermute(value, axis, pairs)


def fold_block(state, queries, keys, values, visible):
    best, total, summed = state
    scores = jnp.einsum(
        "cgqd,kgd->gqck", queries, keys, preferred_element_type=jnp.float32
    ) * HD ** (-0.5)
    shown = visible[None, None, :, :]
    scores = jnp.where(shown, scores, NEG)
    newest = jnp.maximum(best, jnp.max(scores, axis=-1))
    factor = jnp.exp(best - newest)
    weights = jnp.where(shown, jnp.exp(scores - newest[..., None]), 0.0)
    total = total * factor + jnp.sum(weights, axis=-1)
    summed = summed * factor[..., None] + jnp.einsum(
        "gqck,kgd->gqcd", weights.astype(jnp.bfloat16), values, preferred_element_type=jnp.float32
    )
    return (newest, total, summed)


def decode_block(decode_q, decode_cache, decode_new, decode_len, groups):
    rows = decode_q.shape[0]
    length = decode_cache.shape[2]
    queries = decode_q.reshape(rows, groups, QPK, HD)
    keys = decode_cache[0].reshape(rows, length, groups, HD)
    values = decode_cache[1].reshape(rows, length, groups, HD)
    own_key = decode_new[0].reshape(rows, groups, HD)
    own_value = decode_new[1].reshape(rows, groups, HD)
    scale = HD ** (-0.5)
    scores = (
        jnp.einsum("rgqd,rlgd->rgql", queries, keys, preferred_element_type=jnp.float32) * scale
    )
    live = (jnp.arange(length, dtype=jnp.int32)[None, :] < decode_len[:, None])[:, None, None, :]
    own = jnp.einsum("rgqd,rgd->rgq", queries, own_key, preferred_element_type=jnp.float32) * scale
    top = jnp.maximum(jnp.max(jnp.where(live, scores, NEG), axis=-1), own)
    weights = jnp.where(live, jnp.exp(scores - top[..., None]), 0.0)
    own_weight = jnp.exp(own - top)
    own_prob = lax.optimization_barrier(own_weight.astype(jnp.bfloat16)).astype(jnp.float32)
    summed = jnp.einsum(
        "rgql,rlgd->rgqd", weights.astype(jnp.bfloat16), values, preferred_element_type=jnp.float32
    )
    summed = summed + own_prob[..., None] * own_value.astype(jnp.float32)[:, :, None, :]
    result = summed / (jnp.sum(weights, axis=-1) + own_weight)[..., None]
    return result.reshape(rows, groups * QPK * HD).astype(jnp.bfloat16)


def greet(axis, count, me):
    barrier = pltpu.get_barrier_semaphore()
    for step in range(1, count):
        pl.semaphore_signal(
            barrier,
            inc=1,
            device_id={axis: lax.rem(me + step, count)},
            device_id_type=pl.DeviceIdType.MESH,
        )
    pl.semaphore_wait(barrier, count - 1)


def remote(source, target, send, recv, axis, device):
    return pltpu.make_async_remote_copy(
        src_ref=source,
        dst_ref=target,
        send_sem=send,
        recv_sem=recv,
        device_id={axis: device},
        device_id_type=pl.DeviceIdType.MESH,
    )


def exchange_kernel(axis, count, blocks, paired, *refs):
    total = len(blocks) + paired
    ins, outs = refs[:total], refs[total : 2 * total]
    send, recv, local = refs[2 * total :]
    me = lax.axis_index(axis)
    greet(axis, count, me)
    copies = []
    for k in range(len(blocks), total):
        parity = lax.rem(me, 2)
        copies.append(
            remote(
                ins[k].at[1 - parity], outs[k], send.at[0, k], recv.at[0, k], axis, me + 1 - 2 * parity
            )
        )
    for step in range(1, count):
        to = lax.rem(me + step, count)
        for k, amount in enumerate(blocks):
            copies.append(
                remote(
                    ins[k].at[lax.rem(to, amount)],
                    outs[k].at[me],
                    send.at[step, k],
                    recv.at[step, k],
                    axis,
                    to,
                )
            )
    for copy in copies:
        copy.start()
    own = []
    for k, amount in enumerate(blocks):
        own.append(
            pltpu.make_async_copy(ins[k].at[lax.rem(me, amount)], outs[k].at[me], local.at[k])
        )
        own[-1].start()
    for copy in own:
        copy.wait()
    for copy in copies:
        copy.wait()


def exchange(axis, arrays, pairs, collective_id):
    count = lax.axis_size(axis)
    blocks = tuple(a.shape[0] for a in arrays)
    total = len(arrays) + len(pairs)
    shapes = [jax.ShapeDtypeStruct((count,) + a.shape[1:], a.dtype) for a in arrays]
    shapes += [jax.ShapeDtypeStruct(a.shape[1:], a.dtype) for a in pairs]
    return pl.pallas_call(
        functools.partial(exchange_kernel, axis, count, blocks, len(pairs)),
        out_shape=shapes,
        in_specs=[pl.BlockSpec(memory_space=pl.ANY)] * total,
        out_specs=[pl.BlockSpec(memory_space=pl.ANY)] * total,
        scratch_shapes=[
            pltpu.SemaphoreType.DMA((count, total)),
            pltpu.SemaphoreType.DMA((count, total)),
            pltpu.SemaphoreType.DMA((total,)),
        ],
        compiler_params=pltpu.CompilerParams(collective_id=collective_id, has_side_effects=True),
    )(*arrays, *pairs)


def gather_kernel(x, out, send, recv, local):
    me = lax.axis_index("ctx")
    core = lax.rem(me, 2)
    column = lax.rem(me // 2, 2)
    line = me // 4
    buddy = me + 1 - 2 * core
    side = me + 2 - 4 * column
    across = me + 4 - 8 * line
    corner = side + across - me
    greet("ctx", 8, me)

    def relay(k, source, target, device):
        return remote(source, target, send.at[k], recv.at[k], "ctx", device)

    def arrival(k, target):
        return relay(k, target, target, buddy)

    near = [
        relay(0, x, out.at[me], side),
        relay(1, x, out.at[me], across),
        relay(2, x, out.at[me], buddy),
    ]
    for copy in near:
        copy.start()
    own = pltpu.make_async_copy(x, out.at[me], local)
    own.start()
    arrival(0, out.at[side]).wait_recv()
    far = [
        relay(3, out.at[side, 0], out.at[side, 0], across),
        relay(4, out.at[side], out.at[side], buddy),
    ]
    for copy in far:
        copy.start()
    arrival(1, out.at[across]).wait_recv()
    more = [
        relay(5, out.at[across, 1], out.at[across, 1], side),
        relay(6, out.at[across], out.at[across], buddy),
    ]
    for copy in more:
        copy.start()
    arrival(3, out.at[corner, 0]).wait_recv()
    last = [relay(7, out.at[corner, 0], out.at[corner, 0], buddy)]
    last[0].start()
    arrival(5, out.at[corner, 1]).wait_recv()
    last.append(relay(8, out.at[corner, 1], out.at[corner, 1], buddy))
    last[1].start()
    arrival(2, out.at[buddy]).wait_recv()
    arrival(4, out.at[buddy + side - me]).wait_recv()
    arrival(6, out.at[buddy + across - me]).wait_recv()
    arrival(7, out.at[buddy + corner - me, 0]).wait_recv()
    arrival(8, out.at[buddy + corner - me, 1]).wait_recv()
    for copy in near + far + more + last:
        copy.wait_send()
    own.wait()


def gather(x, collective_id):
    return pl.pallas_call(
        gather_kernel,
        out_shape=jax.ShapeDtypeStruct((8,) + x.shape, x.dtype),
        in_specs=[pl.BlockSpec(memory_space=pl.ANY)],
        out_specs=pl.BlockSpec(memory_space=pl.ANY),
        scratch_shapes=[
            pltpu.SemaphoreType.DMA((9,)),
            pltpu.SemaphoreType.DMA((9,)),
            pltpu.SemaphoreType.DMA,
        ],
        compiler_params=pltpu.CompilerParams(collective_id=collective_id, has_side_effects=True),
    )(x)


def part_kernel(rows, tile, q_ref, k_ref, v_ref, place_ref, out_ref, lse_ref):
    source = pl.program_id(0)
    span = place_ref.shape[1]
    plain = k_ref.shape[0] - span
    place = source * rows + lax.broadcasted_iota(jnp.int32, (tile, span), 0) % rows
    shown = place_ref[...] <= place
    for start in range(0, q_ref.shape[1], tile):
        scores = lax.dot_general(
            q_ref[0, start : start + tile, :],
            k_ref[...],
            (((1,), (1,)), ((), ())),
            preferred_element_type=jnp.float32,
        ) * HD ** (-0.5)
        scores = jnp.concatenate(
            [scores[:, :plain], jnp.where(shown, scores[:, plain:], NEG)], axis=1
        )
        top = jnp.max(scores, axis=1, keepdims=True)
        probs = jnp.exp(scores - top).astype(jnp.bfloat16)
        summed = jnp.dot(probs, v_ref[...], preferred_element_type=jnp.float32)
        total = summed[:, HD:]
        out_ref[0, start : start + tile, :] = (summed[:, :HD] / total).astype(jnp.bfloat16)
        lse = (top + jnp.log(total)).T
        lse_ref[0, :, start : start + tile] = lse[:8, :]


def span_parts(queries, keys, values, place, rows):
    count, stacked, _ = queries.shape
    width = keys.shape[0]
    tile = 2 * rows
    return pl.pallas_call(
        functools.partial(part_kernel, rows, tile),
        grid=(count,),
        out_shape=[
            jax.ShapeDtypeStruct((count, stacked, HD), jnp.bfloat16),
            jax.ShapeDtypeStruct((count, 8, stacked), jnp.float32),
        ],
        in_specs=[
            pl.BlockSpec((1, stacked, HD), lambda i: (i, 0, 0)),
            pl.BlockSpec((width, HD), lambda i: (0, 0)),
            pl.BlockSpec((width, 2 * HD), lambda i: (0, 0)),
            pl.BlockSpec((1, place.shape[1]), lambda i: (0, 0)),
        ],
        out_specs=[
            pl.BlockSpec((1, stacked, HD), lambda i: (i, 0, 0)),
            pl.BlockSpec((1, 8, stacked), lambda i: (i, 0, 0)),
        ],
        compiler_params=pltpu.CompilerParams(vmem_limit_bytes=48 * 1024 * 1024),
    )(queries, keys, values, place)


def split_span(span_q, prompt_kv, span_kv):
    rows = span_q.shape[0]
    prompt_rows = prompt_kv.shape[1]
    here = lax.axis_index("ctx")
    core = here % 2
    buddy = here + 1 - 2 * core
    by_group = span_q.reshape(rows, 2, QPK, HD).transpose(1, 2, 0, 3).reshape(2, QPK * rows, HD)
    local_kv = jnp.concatenate([prompt_kv, span_kv], axis=1)
    kv = local_kv.reshape(2, prompt_rows + rows, 2, HD).transpose(2, 0, 1, 3)
    queries, other = exchange("ctx", [by_group], [kv], 0)
    own = jnp.where(core == 0, kv[0], kv[1])
    joined = jnp.concatenate(
        [own[:, :prompt_rows], other[:, :prompt_rows], own[:, prompt_rows:], other[:, prompt_rows:]],
        axis=1,
    )
    spots = jnp.arange(rows, dtype=jnp.int32)
    place = jnp.concatenate([here * rows + spots, buddy * rows + spots])[None, :]
    values = jnp.concatenate([joined[1], jnp.ones_like(joined[1])], axis=1)
    parts, lse = span_parts(queries, joined[0], values, place, rows)
    parts, lse = exchange("ctx", [parts, lse], [], 1)
    lse = lse[:, 0].reshape(-1, 2, QPK, rows)
    weight = jnp.exp(lse - jnp.max(lse, axis=0, keepdims=True))
    weight = weight / jnp.sum(weight, axis=0, keepdims=True)
    parts = parts.reshape(-1, 2, QPK, rows, HD).astype(jnp.float32)
    result = jnp.sum(weight[..., None] * parts, axis=0)
    return result.transpose(2, 0, 1, 3).reshape(rows, 2 * QPK * HD).astype(jnp.bfloat16)


def ring_span(span_q, prompt_kv, span_kv):
    groups = prompt_kv.shape[2] // HD
    span_rows = span_q.shape[0]
    prompt_rows = prompt_kv.shape[1]
    local_width = prompt_rows + span_rows
    loop_size = lax.axis_size("ctx")
    here = lax.axis_index("ctx")
    queries = span_q.reshape(span_rows, groups, QPK, HD)
    local_kv = jnp.concatenate([prompt_kv, span_kv], axis=1)
    keys = local_kv[0].reshape(local_width, groups, HD)
    values = local_kv[1].reshape(local_width, groups, HD)
    query_place = jnp.arange(span_rows, dtype=jnp.int32)
    key_place = jnp.arange(local_width, dtype=jnp.int32)
    empty = (
        jnp.full((groups, QPK, span_rows), NEG, jnp.float32),
        jnp.zeros((groups, QPK, span_rows), jnp.float32),
        jnp.zeros((groups, QPK, span_rows, HD), jnp.float32),
    )

    def visible_from(source):
        span_key = here * span_rows + key_place - prompt_rows
        span_query = source * span_rows + query_place
        return (key_place[None, :] < prompt_rows) | (span_key[None, :] <= span_query[:, None])

    def loop_step(step, carry):
        moving, best, total, summed = carry
        source = (here - step) % loop_size
        best, total, summed = fold_block(
            (best, total, summed), moving, keys, values, visible_from(source)
        )
        moving = from_behind(moving, "ctx", 1)
        best, total, summed = from_behind((best, total, summed), "ctx", 1)
        return (moving, best, total, summed)

    leftover, best, total, summed = lax.fori_loop(0, loop_size, loop_step, (queries,) + empty)
    return (
        (summed / total[..., None])
        .transpose(2, 0, 1, 3)
        .reshape(span_rows, groups * QPK * HD)
        .astype(jnp.bfloat16)
    )


def on_device(
    span_q,
    prompt_kv,
    span_kv,
    decode_q,
    decode_cache,
    decode_new,
    decode_len,
    residual,
    norm_gain,
    router,
    expert_ids,
    capacity,
    w_gate,
    w_up,
    w_down,
):
    groups = prompt_kv.shape[2] // HD
    paired = lax.axis_size("ctx") == 8 and groups == 2
    spread = split_span if paired else ring_span
    span_out = spread(span_q, prompt_kv, span_kv)
    decode_out = decode_block(decode_q, decode_cache, decode_new, decode_len, groups)
    attn = jnp.concatenate([span_out, decode_out], axis=0)
    carried = residual.astype(jnp.float32) + attn.astype(jnp.float32)
    gained = carried * norm_gain.astype(jnp.float32)
    squares = jnp.sum(carried * carried, axis=1)
    partial_logits = jnp.dot(gained, router.astype(jnp.float32), precision=lax.Precision.HIGHEST)
    if paired:
        sums = jnp.concatenate([partial_logits, squares[:, None]], axis=1).T
        sums = jnp.pad(sums, ((0, 16 - sums.shape[0]), (0, -sums.shape[1] % 128)))
        (sums,) = exchange("exp", [sums[None]], [], 2)
        sums = jnp.sum(sums, axis=0)[:, : squares.shape[0]].T
        squares, logits = sums[:, EXPERTS], sums[:, :EXPERTS]
    else:
        squares, logits = lax.psum((squares, partial_logits), "exp")
    rscale = lax.rsqrt(squares / D + EPS)
    logits = logits * rscale[:, None]
    normed = (gained * rscale[:, None]).astype(jnp.bfloat16)
    row_count = expert_ids.shape[0]
    slots = CAP * EXPERTS
    expert_range = jnp.arange(EXPERTS, dtype=jnp.int32)
    onehot = expert_ids[:, :, None] == expert_range[None, None, :]
    chosen = jnp.sum(jnp.where(onehot, logits[:, None, :], 0.0), axis=-1)
    route_weight = jax.nn.sigmoid(chosen - chosen[:, ::-1])
    flat_ids = expert_ids.reshape(row_count * TOPK)
    assign = onehot.reshape(row_count * TOPK, EXPERTS).astype(jnp.int32)
    prior = jnp.cumsum(assign, axis=0) - assign
    position = jnp.sum(prior * assign, axis=1)
    limit = jnp.sum(assign * capacity[None, :], axis=1)
    kept = position < limit
    slot_index = flat_ids * CAP + position
    select = kept[:, None] & (slot_index[:, None] == jnp.arange(slots, dtype=jnp.int32)[None, :])
    select = select.reshape(row_count, TOPK, slots)
    placing = jnp.sum(select.astype(jnp.float32), axis=1).astype(jnp.bfloat16)
    outgoing = jnp.einsum("rs,rd->sd", placing, normed, preferred_element_type=jnp.float32).astype(
        jnp.bfloat16
    )
    features = normed.shape[1]
    owners = lax.axis_size("exp")
    held = EXPERTS // owners
    outgoing = outgoing.reshape(owners, held, CAP, features)
    if paired:
        (arrived,) = exchange("exp", [outgoing], [], 3)
        arrived = arrived.transpose(1, 2, 0, 3).reshape(held, CAP, owners * features)
        piece = gather(arrived, 4)
    else:
        arrived = lax.all_to_all(outgoing, "exp", split_axis=0, concat_axis=3, tiled=True)[0]
        piece = lax.all_gather(arrived, "ctx", axis=0)
    gate = jnp.einsum("necd,edf->encf", piece, w_gate, preferred_element_type=jnp.float32)
    up = jnp.einsum("necd,edf->encf", piece, w_up, preferred_element_type=jnp.float32)
    hidden = (jax.nn.silu(gate) * up).astype(jnp.bfloat16)
    result = lax.psum_scatter(
        jnp.einsum("encf,efd->necd", hidden, w_down, preferred_element_type=jnp.float32).astype(
            jnp.bfloat16
        ),
        "ctx",
        scatter_dimension=0,
        tiled=True,
    )[0]
    if paired:
        result = result.reshape(held, CAP, owners, features).transpose(2, 0, 1, 3)
        (returned,) = exchange("exp", [result], [], 5)
    else:
        returned = lax.all_to_all(result[None], "exp", split_axis=3, concat_axis=0, tiled=True)
    returned = returned.reshape(slots, features).astype(jnp.float32)
    mixing = jnp.sum(select.astype(jnp.float32) * route_weight[:, :, None], axis=1)
    moe = jnp.dot(mixing, returned, precision=lax.Precision.HIGHEST)
    return (carried + moe).astype(jnp.bfloat16)


def solution(mesh):
    placed = (
        P("ctx", "exp"),
        P(None, "ctx", "exp"),
        P(None, "ctx", "exp"),
        P("ctx", "exp"),
        P(None, "ctx", None, "exp"),
        P(None, "ctx", "exp"),
        P("ctx"),
        P("ctx", "exp"),
        P("exp"),
        P("exp", None),
        P("ctx", None),
        P(),
        P("exp", None, "ctx"),
        P("exp", None, "ctx"),
        P("exp", "ctx", None),
    )
    return jax.shard_map(
        on_device, mesh=mesh, in_specs=placed, out_specs=P("ctx", "exp"), check_vma=False
    )
```

```python
import functools

import jax
import jax.numpy as jnp
from jax import lax
from jax.experimental import pallas as pl
from jax.experimental.pallas import tpu as pltpu
from jax.sharding import PartitionSpec as P

D = 6144
HD = 128
QPK = 6
EXPERTS = 8
TOPK = 2
CAP = 40


NEG = -1e30
EPS = 1e-05


def from_behind(value, axis, steps):
    count = lax.axis_size(axis)
    pairs = [(source, (source + steps) % count) for source in range(count)]
    return lax.ppermute(value, axis, pairs)


def fold_block(state, queries, keys, values, visible):
    best, total, summed = state
    scores = jnp.einsum(
        "cgqd,kgd->gqck", queries, keys, preferred_element_type=jnp.float32
    ) * HD ** (-0.5)
    shown = visible[None, None, :, :]
    scores = jnp.where(shown, scores, NEG)
    newest = jnp.maximum(best, jnp.max(scores, axis=-1))
    factor = jnp.exp(best - newest)
    weights = jnp.where(shown, jnp.exp(scores - newest[..., None]), 0.0)
    total = total * factor + jnp.sum(weights, axis=-1)
    summed = summed * factor[..., None] + jnp.einsum(
        "gqck,kgd->gqcd", weights.astype(jnp.bfloat16), values, preferred_element_type=jnp.float32
    )
    return (newest, total, summed)


def decode_block(decode_q, decode_cache, decode_new, decode_len, groups):
    rows = decode_q.shape[0]
    length = decode_cache.shape[2]
    queries = decode_q.reshape(rows, groups, QPK, HD)
    keys = decode_cache[0].reshape(rows, length, groups, HD)
    values = decode_cache[1].reshape(rows, length, groups, HD)
    own_key = decode_new[0].reshape(rows, groups, HD)
    own_value = decode_new[1].reshape(rows, groups, HD)
    scale = HD ** (-0.5)
    scores = (
        jnp.einsum("rgqd,rlgd->rgql", queries, keys, preferred_element_type=jnp.float32) * scale
    )
    live = (jnp.arange(length, dtype=jnp.int32)[None, :] < decode_len[:, None])[:, None, None, :]
    own = jnp.einsum("rgqd,rgd->rgq", queries, own_key, preferred_element_type=jnp.float32) * scale
    top = jnp.maximum(jnp.max(jnp.where(live, scores, NEG), axis=-1), own)
    weights = jnp.where(live, jnp.exp(scores - top[..., None]), 0.0)
    own_weight = jnp.exp(own - top)
    own_prob = lax.optimization_barrier(own_weight.astype(jnp.bfloat16)).astype(jnp.float32)
    summed = jnp.einsum(
        "rgql,rlgd->rgqd", weights.astype(jnp.bfloat16), values, preferred_element_type=jnp.float32
    )
    summed = summed + own_prob[..., None] * own_value.astype(jnp.float32)[:, :, None, :]
    result = summed / (jnp.sum(weights, axis=-1) + own_weight)[..., None]
    return result.reshape(rows, groups * QPK * HD).astype(jnp.bfloat16)


def greet(axis, count, me):
    barrier = pltpu.get_barrier_semaphore()
    for step in range(1, count):
        pl.semaphore_signal(
            barrier,
            inc=1,
            device_id={axis: lax.rem(me + step, count)},
            device_id_type=pl.DeviceIdType.MESH,
        )
    pl.semaphore_wait(barrier, count - 1)


def remote(source, target, send, recv, axis, device):
    return pltpu.make_async_remote_copy(
        src_ref=source,
        dst_ref=target,
        send_sem=send,
        recv_sem=recv,
        device_id={axis: device},
        device_id_type=pl.DeviceIdType.MESH,
    )


def exchange_kernel(axis, count, blocks, paired, *refs):
    total = len(blocks) + paired
    ins, outs = refs[:total], refs[total : 2 * total]
    send, recv, local = refs[2 * total :]
    me = lax.axis_index(axis)
    greet(axis, count, me)
    copies = []
    for k in range(len(blocks), total):
        parity = lax.rem(me, 2)
        copies.append(
            remote(
                ins[k].at[1 - parity], outs[k], send.at[0, k], recv.at[0, k], axis, me + 1 - 2 * parity
            )
        )
    for step in range(1, count):
        to = lax.rem(me + step, count)
        for k, amount in enumerate(blocks):
            copies.append(
                remote(
                    ins[k].at[lax.rem(to, amount)],
                    outs[k].at[me],
                    send.at[step, k],
                    recv.at[step, k],
                    axis,
                    to,
                )
            )
    for copy in copies:
        copy.start()
    own = []
    for k, amount in enumerate(blocks):
        own.append(
            pltpu.make_async_copy(ins[k].at[lax.rem(me, amount)], outs[k].at[me], local.at[k])
        )
        own[-1].start()
    for copy in own:
        copy.wait()
    for copy in copies:
        copy.wait()


def exchange(axis, arrays, pairs, collective_id):
    count = lax.axis_size(axis)
    blocks = tuple(a.shape[0] for a in arrays)
    total = len(arrays) + len(pairs)
    shapes = [jax.ShapeDtypeStruct((count,) + a.shape[1:], a.dtype) for a in arrays]
    shapes += [jax.ShapeDtypeStruct(a.shape[1:], a.dtype) for a in pairs]
    return pl.pallas_call(
        functools.partial(exchange_kernel, axis, count, blocks, len(pairs)),
        out_shape=shapes,
        in_specs=[pl.BlockSpec(memory_space=pl.ANY)] * total,
        out_specs=[pl.BlockSpec(memory_space=pl.ANY)] * total,
        scratch_shapes=[
            pltpu.SemaphoreType.DMA((count, total)),
            pltpu.SemaphoreType.DMA((count, total)),
            pltpu.SemaphoreType.DMA((total,)),
        ],
        compiler_params=pltpu.CompilerParams(collective_id=collective_id, has_side_effects=True),
    )(*arrays, *pairs)


def gather_kernel(x, out, send, recv, local):
    me = lax.axis_index("ctx")
    core = lax.rem(me, 2)
    column = lax.rem(me // 2, 2)
    line = me // 4
    buddy = me + 1 - 2 * core
    side = me + 2 - 4 * column
    across = me + 4 - 8 * line
    corner = side + across - me
    greet("ctx", 8, me)

    def relay(k, source, target, device):
        return remote(source, target, send.at[k], recv.at[k], "ctx", device)

    def arrival(k, target):
        return relay(k, target, target, buddy)

    near = [
        relay(0, x, out.at[me], side),
        relay(1, x, out.at[me], across),
        relay(2, x, out.at[me], buddy),
    ]
    for copy in near:
        copy.start()
    own = pltpu.make_async_copy(x, out.at[me], local)
    own.start()
    arrival(0, out.at[side]).wait_recv()
    far = [
        relay(3, out.at[side, 0], out.at[side, 0], across),
        relay(4, out.at[side], out.at[side], buddy),
    ]
    for copy in far:
        copy.start()
    arrival(1, out.at[across]).wait_recv()
    more = [
        relay(5, out.at[across, 1], out.at[across, 1], side),
        relay(6, out.at[across], out.at[across], buddy),
    ]
    for copy in more:
        copy.start()
    arrival(3, out.at[corner, 0]).wait_recv()
    last = [relay(7, out.at[corner, 0], out.at[corner, 0], buddy)]
    last[0].start()
    arrival(5, out.at[corner, 1]).wait_recv()
    last.append(relay(8, out.at[corner, 1], out.at[corner, 1], buddy))
    last[1].start()
    arrival(2, out.at[buddy]).wait_recv()
    arrival(4, out.at[buddy + side - me]).wait_recv()
    arrival(6, out.at[buddy + across - me]).wait_recv()
    arrival(7, out.at[buddy + corner - me, 0]).wait_recv()
    arrival(8, out.at[buddy + corner - me, 1]).wait_recv()
    for copy in near + far + more + last:
        copy.wait_send()
    own.wait()


def gather(x, collective_id):
    return pl.pallas_call(
        gather_kernel,
        out_shape=jax.ShapeDtypeStruct((8,) + x.shape, x.dtype),
        in_specs=[pl.BlockSpec(memory_space=pl.ANY)],
        out_specs=pl.BlockSpec(memory_space=pl.ANY),
        scratch_shapes=[
            pltpu.SemaphoreType.DMA((9,)),
            pltpu.SemaphoreType.DMA((9,)),
            pltpu.SemaphoreType.DMA,
        ],
        compiler_params=pltpu.CompilerParams(collective_id=collective_id, has_side_effects=True),
    )(x)


def part_kernel(rows, tile, q_ref, k_ref, v_ref, place_ref, out_ref, lse_ref):
    source = pl.program_id(0)
    span = place_ref.shape[1]
    plain = k_ref.shape[0] - span
    place = source * rows + lax.broadcasted_iota(jnp.int32, (tile, span), 0) % rows
    shown = place_ref[...] <= place
    for start in range(0, q_ref.shape[1], tile):
        scores = lax.dot_general(
            q_ref[0, start : start + tile, :],
            k_ref[...],
            (((1,), (1,)), ((), ())),
            preferred_element_type=jnp.float32,
        ) * HD ** (-0.5)
        scores = jnp.concatenate(
            [scores[:, :plain], jnp.where(shown, scores[:, plain:], NEG)], axis=1
        )
        top = jnp.max(scores, axis=1, keepdims=True)
        probs = jnp.exp(scores - top).astype(jnp.bfloat16)
        summed = jnp.dot(probs, v_ref[...], preferred_element_type=jnp.float32)
        total = summed[:, HD:]
        out_ref[0, start : start + tile, :] = (summed[:, :HD] / total).astype(jnp.bfloat16)
        lse = (top + jnp.log(total)).T
        lse_ref[0, :, start : start + tile] = lse[:8, :]


def span_parts(queries, keys, values, place, rows):
    count, stacked, _ = queries.shape
    width = keys.shape[0]
    tile = 2 * rows
    return pl.pallas_call(
        functools.partial(part_kernel, rows, tile),
        grid=(count,),
        out_shape=[
            jax.ShapeDtypeStruct((count, stacked, HD), jnp.bfloat16),
            jax.ShapeDtypeStruct((count, 8, stacked), jnp.float32),
        ],
        in_specs=[
            pl.BlockSpec((1, stacked, HD), lambda i: (i, 0, 0)),
            pl.BlockSpec((width, HD), lambda i: (0, 0)),
            pl.BlockSpec((width, 2 * HD), lambda i: (0, 0)),
            pl.BlockSpec((1, place.shape[1]), lambda i: (0, 0)),
        ],
        out_specs=[
            pl.BlockSpec((1, stacked, HD), lambda i: (i, 0, 0)),
            pl.BlockSpec((1, 8, stacked), lambda i: (i, 0, 0)),
        ],
        compiler_params=pltpu.CompilerParams(vmem_limit_bytes=48 * 1024 * 1024),
    )(queries, keys, values, place)


def split_span(span_q, prompt_kv, span_kv):
    rows = span_q.shape[0]
    prompt_rows = prompt_kv.shape[1]
    here = lax.axis_index("ctx")
    core = here % 2
    buddy = here + 1 - 2 * core
    by_group = span_q.reshape(rows, 2, QPK, HD).transpose(1, 2, 0, 3).reshape(2, QPK * rows, HD)
    local_kv = jnp.concatenate([prompt_kv, span_kv], axis=1)
    kv = local_kv.reshape(2, prompt_rows + rows, 2, HD).transpose(2, 0, 1, 3)
    queries, other = exchange("ctx", [by_group], [kv], 0)
    own = jnp.where(core == 0, kv[0], kv[1])
    joined = jnp.concatenate(
        [own[:, :prompt_rows], other[:, :prompt_rows], own[:, prompt_rows:], other[:, prompt_rows:]],
        axis=1,
    )
    spots = jnp.arange(rows, dtype=jnp.int32)
    place = jnp.concatenate([here * rows + spots, buddy * rows + spots])[None, :]
    values = jnp.concatenate([joined[1], jnp.ones_like(joined[1])], axis=1)
    parts, lse = span_parts(queries, joined[0], values, place, rows)
    parts, lse = exchange("ctx", [parts, lse], [], 1)
    lse = lse[:, 0].reshape(-1, 2, QPK, rows)
    weight = jnp.exp(lse - jnp.max(lse, axis=0, keepdims=True))
    weight = weight / jnp.sum(weight, axis=0, keepdims=True)
    parts = parts.reshape(-1, 2, QPK, rows, HD).astype(jnp.float32)
    result = jnp.sum(weight[..., None] * parts, axis=0)
    return result.transpose(2, 0, 1, 3).reshape(rows, 2 * QPK * HD).astype(jnp.bfloat16)


def ring_span(span_q, prompt_kv, span_kv):
    groups = prompt_kv.shape[2] // HD
    span_rows = span_q.shape[0]
    prompt_rows = prompt_kv.shape[1]
    local_width = prompt_rows + span_rows
    loop_size = lax.axis_size("ctx")
    here = lax.axis_index("ctx")
    queries = span_q.reshape(span_rows, groups, QPK, HD)
    local_kv = jnp.concatenate([prompt_kv, span_kv], axis=1)
    keys = local_kv[0].reshape(local_width, groups, HD)
    values = local_kv[1].reshape(local_width, groups, HD)
    query_place = jnp.arange(span_rows, dtype=jnp.int32)
    key_place = jnp.arange(local_width, dtype=jnp.int32)
    empty = (
        jnp.full((groups, QPK, span_rows), NEG, jnp.float32),
        jnp.zeros((groups, QPK, span_rows), jnp.float32),
        jnp.zeros((groups, QPK, span_rows, HD), jnp.float32),
    )

    def visible_from(source):
        span_key = here * span_rows + key_place - prompt_rows
        span_query = source * span_rows + query_place
        return (key_place[None, :] < prompt_rows) | (span_key[None, :] <= span_query[:, None])

    def loop_step(step, carry):
        moving, best, total, summed = carry
        source = (here - step) % loop_size
        best, total, summed = fold_block(
            (best, total, summed), moving, keys, values, visible_from(source)
        )
        moving = from_behind(moving, "ctx", 1)
        best, total, summed = from_behind((best, total, summed), "ctx", 1)
        return (moving, best, total, summed)

    leftover, best, total, summed = lax.fori_loop(0, loop_size, loop_step, (queries,) + empty)
    return (
        (summed / total[..., None])
        .transpose(2, 0, 1, 3)
        .reshape(span_rows, groups * QPK * HD)
        .astype(jnp.bfloat16)
    )


def on_device(
    span_q,
    prompt_kv,
    span_kv,
    decode_q,
    decode_cache,
    decode_new,
    decode_len,
    residual,
    norm_gain,
    router,
    expert_ids,
    capacity,
    w_gate,
    w_up,
    w_down,
):
    groups = prompt_kv.shape[2] // HD
    paired = lax.axis_size("ctx") == 8 and groups == 2
    spread = split_span if paired else ring_span
    span_out = spread(span_q, prompt_kv, span_kv)
    decode_out = decode_block(decode_q, decode_cache, decode_new, decode_len, groups)
    attn = jnp.concatenate([span_out, decode_out], axis=0)
    carried = residual.astype(jnp.float32) + attn.astype(jnp.float32)
    gained = carried * norm_gain.astype(jnp.float32)
    squares = jnp.sum(carried * carried, axis=1)
    partial_logits = jnp.dot(gained, router.astype(jnp.float32), precision=lax.Precision.HIGHEST)
    if paired:
        sums = jnp.concatenate([partial_logits, squares[:, None]], axis=1).T
        sums = jnp.pad(sums, ((0, 16 - sums.shape[0]), (0, -sums.shape[1] % 128)))
        (sums,) = exchange("exp", [sums[None]], [], 2)
        sums = jnp.sum(sums, axis=0)[:, : squares.shape[0]].T
        squares, logits = sums[:, EXPERTS], sums[:, :EXPERTS]
    else:
        squares, logits = lax.psum((squares, partial_logits), "exp")
    rscale = lax.rsqrt(squares / D + EPS)
    logits = logits * rscale[:, None]
    normed = (gained * rscale[:, None]).astype(jnp.bfloat16)
    row_count = expert_ids.shape[0]
    slots = CAP * EXPERTS
    expert_range = jnp.arange(EXPERTS, dtype=jnp.int32)
    onehot = expert_ids[:, :, None] == expert_range[None, None, :]
    chosen = jnp.sum(jnp.where(onehot, logits[:, None, :], 0.0), axis=-1)
    route_weight = jax.nn.sigmoid(chosen - chosen[:, ::-1])
    flat_ids = expert_ids.reshape(row_count * TOPK)
    assign = onehot.reshape(row_count * TOPK, EXPERTS).astype(jnp.int32)
    prior = jnp.cumsum(assign, axis=0) - assign
    position = jnp.sum(prior * assign, axis=1)
    limit = jnp.sum(assign * capacity[None, :], axis=1)
    kept = position < limit
    slot_index = flat_ids * CAP + position
    select = kept[:, None] & (slot_index[:, None] == jnp.arange(slots, dtype=jnp.int32)[None, :])
    select = select.reshape(row_count, TOPK, slots)
    placing = jnp.sum(select.astype(jnp.float32), axis=1).astype(jnp.bfloat16)
    outgoing = jnp.einsum("rs,rd->sd", placing, normed, preferred_element_type=jnp.float32).astype(
        jnp.bfloat16
    )
    features = normed.shape[1]
    owners = lax.axis_size("exp")
    held = EXPERTS // owners
    outgoing = outgoing.reshape(owners, held, CAP, features)
    if paired:
        (arrived,) = exchange("exp", [outgoing], [], 3)
        arrived = arrived.transpose(1, 2, 0, 3).reshape(held, CAP, owners * features)
        piece = gather(arrived, 4)
    else:
        arrived = lax.all_to_all(outgoing, "exp", split_axis=0, concat_axis=3, tiled=True)[0]
        piece = lax.all_gather(arrived, "ctx", axis=0)
    gate = jnp.einsum("necd,edf->encf", piece, w_gate, preferred_element_type=jnp.float32)
    up = jnp.einsum("necd,edf->encf", piece, w_up, preferred_element_type=jnp.float32)
    hidden = (jax.nn.silu(gate) * up).astype(jnp.bfloat16)
    parts = jnp.einsum("encf,efd->nced", hidden, w_down, preferred_element_type=jnp.float32)
    parts = parts.astype(jnp.bfloat16).reshape(-1, held, owners * features)
    result = lax.psum_scatter(parts, "ctx", scatter_dimension=0, tiled=True).transpose(1, 0, 2)
    if paired:
        result = result.reshape(held, CAP, owners, features).transpose(2, 0, 1, 3)
        (returned,) = exchange("exp", [result], [], 5)
    else:
        returned = lax.all_to_all(result[None], "exp", split_axis=3, concat_axis=0, tiled=True)
    returned = returned.reshape(slots, features).astype(jnp.float32)
    mixing = jnp.sum(select.astype(jnp.float32) * route_weight[:, :, None], axis=1)
    moe = jnp.dot(mixing, returned, precision=lax.Precision.HIGHEST)
    return (carried + moe).astype(jnp.bfloat16)


def solution(mesh):
    placed = (
        P("ctx", "exp"),
        P(None, "ctx", "exp"),
        P(None, "ctx", "exp"),
        P("ctx", "exp"),
        P(None, "ctx", None, "exp"),
        P(None, "ctx", "exp"),
        P("ctx"),
        P("ctx", "exp"),
        P("exp"),
        P("exp", None),
        P("ctx", None),
        P(),
        P("exp", None, "ctx"),
        P("exp", None, "ctx"),
        P("exp", "ctx", None),
    )
    return jax.shard_map(
        on_device, mesh=mesh, in_specs=placed, out_specs=P("ctx", "exp"), check_vma=False
    )
```
